32 devices in a mesh: gx: 4 (over z), gy: 8 (over y, x, core).
Axes of the slice: x: 2, y: 2, z: 4, core: 2. Of those that a mesh axis runs over, the one named last changes fastest.
Arguments:
- increments: float32 [2, 3, 192, 1024], P(None, None, 'gy', 'gx'), may hold values from -6 to 6
- diffusivity: float32 [3, 192, 1024], P(None, 'gy', 'gx'), may hold values from 0.02 to 0.24
- sea_mask: int32 [192, 1024], P('gy', 'gx'), may hold values 0 or 1
- source_cells: int32 [32, 32, 3, 8, 128], P(('gx', 'gy')), may hold values from 0 to 255, as said below
- source_weights: float32 [32, 32, 8, 128], P(('gx', 'gy')), may hold values from 0.1 to 1
- source_counts: int32 [32, 32, 128], P(('gx', 'gy')), may hold values from 0 to 8
- slot_owner: int32 [32, 32, 128], P(('gx', 'gy')), may hold values from 0 to 4095
Outputs:
- smoothed: float32 [2, 3, 192, 1024], P(None, None, 'gy', 'gx')
- obs_equiv: float32 [131072], P(('gx', 'gy'))
The draws below stay inside these ranges and needn't reach their ends.
Inputs may be any that keep to these rules, and one draw needn't show every extreme that they name: `source_cells`: component 0 is a layer below 6, component 1 a row below 24, component 2 a column below 256, all within the grid device's own tile. `source_counts`: number of leading valid entries of the slot; 0 leaves the slot empty. `slot_owner`: an observation index local to the owner.
All inputs are finite; a program needn't handle non-finite values. No bound on the sum of `sea_mask` on one device may be relied on, other than what follows from the above.
Results may differ from the reference program's by a relative error of at most 0.00002.
Values sent between devices are 32-bit elements; how exact they have to be, the bound alone decides.
A program may use at most 64 MiB of HBM per device.

```python
import math
import jax
import jax.numpy as jnp
from jax import lax

FIELDS = 2
LEVELS = 3
ITERS = 10
CY = 24
CX = 256
OBS_DEV = 4096
SLOTS = 128
NY = 192
NX = 1024
NOBS = 131072
N_GY = 8
DEVICES = 32


def draw_source_cells(key, part):
    key_layer, key_row, key_col = jax.random.split(key, 3)
    shape = (DEVICES, DEVICES, 1, 8, SLOTS)
    layer = jax.random.randint(key_layer, shape, 0, FIELDS * LEVELS, dtype=jnp.int32)
    row_pick = jax.random.randint(key_row, shape, 0, CY, dtype=jnp.int32)
    col_pick = jax.random.randint(key_col, shape, 0, CX, dtype=jnp.int32)
    return jnp.concatenate([layer, row_pick, col_pick], axis=2)


def with_ends(entries, rng, low, largest):
    extent = entries.shape
    spot = [jax.random.randint(jax.random.fold_in(rng, axis), (), 0, extent[axis]) for axis in range(len(extent))]
    entries = entries.at[tuple(spot)].set(low)
    longest = extent.index(max(extent))
    spot[longest] = (spot[longest] + 1) % extent[longest]
    return entries.at[tuple(spot)].set(largest)


def block_scale(own_key, dims, cuts, least, top_value):
    level = 1.0
    for dim, parts in cuts:
        steps = jax.random.uniform(jax.random.fold_in(jax.random.fold_in(own_key, 6), dim), (parts,), jnp.float32, least / len(cuts), top_value / len(cuts))
        level = level * jnp.repeat(jnp.exp(steps), dims[dim] // parts).reshape((-1,) + (1,) * (len(dims) - 1 - dim))
    return level


def centred(own_key, dims, deviation, limit, cuts=(), held_as=jnp.bfloat16):
    values = deviation * jax.random.normal(own_key, dims, jnp.float32)
    if cuts:
        values = values * block_scale(own_key, dims, cuts, -0.22, 0.18)
    return jnp.clip(values, -limit, limit).astype(held_as)


def setup_inputs(seed: int = 0) -> dict:
    arg_keys = jax.random.split(jax.random.key(seed), 8)
    increments = centred(arg_keys[0], (FIELDS, LEVELS, NY, NX), 1.0, 6.0, ((2, 8), (3, 4)), jnp.float32)
    diffusivity = jnp.clip(jnp.exp(math.log(0.24) - 2.4849066 * jax.random.uniform(arg_keys[1], (LEVELS, NY, NX), jnp.float32) ** block_scale(arg_keys[1], (LEVELS, NY, NX), ((1, 8), (2, 4)), -0.2, 0.2)), 0.02, 0.24)
    sea_mask = with_ends((jax.random.randint(arg_keys[2], (NY, NX), 0, 10) < 7).astype(jnp.int32), jax.random.fold_in(arg_keys[2], 1), 0, 1)
    source_cells = draw_source_cells(jax.random.fold_in(arg_keys[7], 71), 0)
    source_weights = jnp.clip(0.1 + 0.9 * jax.random.uniform(arg_keys[4], (DEVICES, DEVICES, 8, SLOTS), jnp.float32) ** block_scale(arg_keys[4], (DEVICES, DEVICES, 8, SLOTS), ((0, 32),), -0.2, 0.2), 0.1, 1.0)
    source_counts = with_ends(jax.random.randint(arg_keys[5], (DEVICES, DEVICES, SLOTS), 0, 9), jax.random.fold_in(arg_keys[5], 1), 0, 8).astype(jnp.int32)
    slot_owner = with_ends(jax.random.randint(arg_keys[6], (DEVICES, DEVICES, SLOTS), 0, OBS_DEV), jax.random.fold_in(arg_keys[6], 1), 0, OBS_DEV - 1).astype(jnp.int32)
    return dict(increments=increments, diffusivity=diffusivity, sea_mask=sea_mask, source_cells=source_cells, source_weights=source_weights, source_counts=source_counts, slot_owner=slot_owner)


def shift_east(array):
    return jnp.roll(array, -1, axis=-1)


def shift_west(array):
    return jnp.roll(array, 1, axis=-1)


def shift_north(array):
    return jnp.concatenate([array[..., 1:, :], jnp.zeros_like(array[..., :1, :])], axis=-2)


def shift_south(array):
    return jnp.concatenate([jnp.zeros_like(array[..., :1, :]), array[..., :-1, :]], axis=-2)


def reference(increments, diffusivity, sea_mask, source_cells, source_weights, source_counts, slot_owner):
    wet = sea_mask.astype(jnp.float32)

    def smooth_level(pair):
        level_fields, diffuse = pair
        c_east = 0.5 * (diffuse + shift_east(diffuse)) * wet * shift_east(wet)
        c_west = 0.5 * (diffuse + shift_west(diffuse)) * wet * shift_west(wet)
        c_north = 0.5 * (diffuse + shift_north(diffuse)) * wet * shift_north(wet)
        c_south = 0.5 * (diffuse + shift_south(diffuse)) * wet * shift_south(wet)
        field = level_fields * wet
        for turn_index in range(ITERS):
            field = field + (c_east * (shift_east(field) - field) - c_west * (field - shift_west(field))) + (c_north * (shift_north(field) - field) - c_south * (field - shift_south(field)))
        return field

    by_level = lax.map(smooth_level, (jnp.transpose(increments, (1, 0, 2, 3)), diffusivity))
    smoothed = jnp.transpose(by_level, (1, 0, 2, 3))
    device_ids = jnp.arange(DEVICES, dtype=jnp.int32)[:, None, None, None]
    lon_block = device_ids // N_GY
    lat_block = device_ids % N_GY
    layer = source_cells[:, :, 0]
    row_index = source_cells[:, :, 1]
    col_index = source_cells[:, :, 2]
    global_flat = layer * (NY * NX) + (lat_block * CY + row_index) * NX + lon_block * CX + col_index
    values = smoothed.reshape(-1)[global_flat.astype(jnp.int32)]
    valid = jnp.arange(8, dtype=jnp.int32)[None, None, :, None] < source_counts[:, :, None, :]
    partial_value = jnp.sum(jnp.where(valid, source_weights * values, jnp.float32(0.0)), axis=2)
    owner_ids = jnp.arange(DEVICES, dtype=jnp.int32)[:, None, None]
    targets = owner_ids * OBS_DEV + slot_owner
    obs_equiv = jnp.zeros((NOBS,), jnp.float32).at[targets.reshape(-1)].add(jnp.transpose(partial_value, (1, 0, 2)).reshape(-1))
    return smoothed, obs_equiv
```

```python
import functools

import jax
import jax.numpy as jnp
from jax import lax
from jax.experimental import pallas as pl
from jax.experimental.pallas import tpu as pltpu
from jax.sharding import PartitionSpec as P

ITERS = 10
OBS_DEV = 4096
LANES = 128
EDGE = 12
MESH = pl.DeviceIdType.MESH
GROUP = 8


def kernel(
    nx, ny, inc, dif, mask, cells, weights, counts, owner, smoothed, obs,
    ext, c_east, c_north, to_prev, to_next, first_cols, last_cols,
    from_prev, from_next, east_mid, east_next, east_prev, west_mid, west_next, west_prev,
    table, part, recv, halo_send, halo_recv, part_send, part_recv,
):
    nfields, nlevels, rows, cols = inc.shape
    layers = nfields * nlevels
    total = layers + nlevels + 1
    high, wide = ext.shape[1:]
    devices = nx * ny
    gx, gy = lax.axis_index("gx"), lax.axis_index("gy")
    me = gx * ny + gy

    def place(step):
        other = lax.rem(me + step, devices)
        return other, (lax.div(other, ny), lax.rem(other, ny))

    barrier = pltpu.get_barrier_semaphore()

    def greet(step, carry):
        pl.semaphore_signal(barrier, inc=1, device_id=place(step)[1], device_id_type=MESH)
        return carry

    lax.fori_loop(1, devices, greet, 0)

    lane = lax.broadcasted_iota(jnp.int32, (rows, LANES), 1)
    wet = mask[...].astype(jnp.float32)
    packed_first = jnp.zeros((rows, LANES), jnp.float32)
    packed_last = jnp.zeros((rows, LANES), jnp.float32)
    for k in range(total):
        if k < layers:
            value = inc[k // nlevels, k % nlevels] * wet
        elif k < layers + nlevels:
            value = dif[k - layers]
        else:
            value = wet
        ext[k, 0:rows, 0:cols] = value
        ext[k, 32:40, 0:cols] = jnp.zeros((8, cols), jnp.float32)
        to_next[ITERS * k : ITERS * (k + 1), :] = value[rows - ITERS : rows]
        to_prev[ITERS * k : ITERS * (k + 1), :] = value[0:ITERS]
        here = (lane >= EDGE * k) & (lane < EDGE * (k + 1))
        first = value[:, 0:LANES]
        last = value[:, cols - LANES : cols]
        if k:
            first = pltpu.roll(first, EDGE * k, 1)
        last = pltpu.roll(last, (EDGE * k + EDGE) % LANES, 1)
        packed_first = jnp.where(here, first, packed_first)
        packed_last = jnp.where(here, last, packed_last)
    first_cols[...] = packed_first
    last_cols[...] = packed_last

    pl.semaphore_wait(barrier, devices - 1)

    east, west = lax.rem(gx + 1, nx), lax.rem(gx + nx - 1, nx)
    north, south = lax.rem(gy + 1, ny), lax.rem(gy + ny - 1, ny)
    plan = [
        (to_next, from_prev, (gx, north)),
        (to_prev, from_next, (gx, south)),
        (first_cols, east_mid, (west, gy)),
        (last_cols, west_mid, (east, gy)),
        (first_cols.at[0:16], east_next, (west, south)),
        (first_cols.at[8:24], east_prev, (west, north)),
        (last_cols.at[0:16], west_next, (east, south)),
        (last_cols.at[8:24], west_prev, (east, north)),
    ]
    copies = [
        pltpu.make_async_remote_copy(
            src_ref=src, dst_ref=dst, send_sem=halo_send.at[i], recv_sem=halo_recv.at[i],
            device_id=target, device_id_type=MESH,
        )
        for i, (src, dst, target) in enumerate(plan)
    ]
    for copy in copies:
        copy.start()

    for copy in copies[2:]:
        copy.wait_recv()
    sub = lax.broadcasted_iota(jnp.int32, (8, LANES), 0)
    lane48 = lax.broadcasted_iota(jnp.int32, (high, LANES), 1)

    def stack(mid, after, before):
        return jnp.concatenate(
            [mid[...], after[0:8], jnp.where(sub < 4, after[8:16], before[0:8]), before[8:16]], axis=0
        )

    east_all = stack(east_mid, east_next, east_prev)
    west_all = stack(west_mid, west_next, west_prev)
    for k in range(total):
        right = pltpu.roll(east_all, (LANES - EDGE * k) % LANES, 1) if k else east_all
        left = pltpu.roll(west_all, (2 * LANES - EDGE - EDGE * k) % LANES, 1)
        ext[k, :, cols:wide] = jnp.where(lane48 < LANES // 2, right, left)
    for copy in copies[:2]:
        copy.wait_recv()
    for k in range(total):
        ext[k, rows : rows + ITERS, 0:cols] = from_next[ITERS * k : ITERS * (k + 1), :]
        ext[k, high - ITERS : high, 0:cols] = from_prev[ITERS * k : ITERS * (k + 1), :]
    row_id = lax.broadcasted_iota(jnp.int32, (high, wide), 0)
    lowest = jnp.where(gy == 0, 36, high)
    highest = jnp.where(gy == ny - 1, rows, 36)
    outside = ((row_id >= highest) & (row_id < 36)) | (row_id >= lowest)
    wet_all = jnp.where(outside, 0.0, ext[total - 1])

    def up(array, axis):
        return pltpu.roll(array, array.shape[axis] - 1, axis)

    wet_east = wet_all * up(wet_all, 1)
    wet_north = wet_all * up(wet_all, 0)
    for level in range(nlevels):
        diffuse = ext[layers + level]
        c_east[level] = 0.5 * (diffuse + up(diffuse, 1)) * wet_east
        c_north[level] = 0.5 * (diffuse + up(diffuse, 0)) * wet_north
    for level in range(nlevels):

        def advance(_, fields):
            ce, cn = c_east[level], c_north[level]
            out = []
            for f in fields:
                flux_e = ce * (up(f, 1) - f)
                flux_n = cn * (up(f, 0) - f)
                f = f + (flux_e - pltpu.roll(flux_e, 1, 1)) + (flux_n - pltpu.roll(flux_n, 1, 0))
                out.append(f)
            return tuple(out)

        fields = lax.fori_loop(
            0, ITERS, advance, tuple(ext[f * nlevels + level] for f in range(nfields))
        )
        for f in range(nfields):
            k = f * nlevels + level
            smoothed[f, level] = fields[f][0:rows, 0:cols]
            for half in range(cols // LANES):
                at = (half * layers + k) * rows
                table[at : at + rows, :] = fields[f][0:rows, half * LANES : (half + 1) * LANES]
    for copy in copies:
        copy.wait_send()

    slot = lax.broadcasted_iota(jnp.int32, (8, LANES), 0)

    def look_up(group, carry):
        at = [group * GROUP + i for i in range(GROUP)]
        lanes = [cells[0, o, 2] & (LANES - 1) for o in at]
        wanted = [
            (lax.shift_right_logical(cells[0, o, 2], 7) * layers + cells[0, o, 0]) * rows
            + cells[0, o, 1]
            for o in at
        ]

        def scan(step, found):
            for i in range(8):
                r = step * 8 + i
                line = jnp.broadcast_to(table[pl.ds(r, 1), :], (8, LANES))
                found = tuple(
                    jnp.where(
                        w == r,
                        jnp.take_along_axis(line, l, axis=1, mode="promise_in_bounds"),
                        have,
                    )
                    for w, l, have in zip(wanted, lanes, found)
                )
            return found

        zero = jnp.zeros((8, LANES), jnp.float32)
        found = lax.fori_loop(0, table.shape[0] // 8, scan, (zero,) * GROUP)
        for o, value in zip(at, found):
            keep = slot < counts[0, pl.ds(o, 1), :]
            part[o] = jnp.sum(
                jnp.where(keep, weights[0, o] * value, 0.0), axis=0, keepdims=True
            )
        return carry

    lax.fori_loop(0, devices // GROUP, look_up, 0)

    def send(step, carry):
        other, target = place(step)
        pltpu.make_async_remote_copy(
            src_ref=part.at[other], dst_ref=recv.at[me], send_sem=part_send, recv_sem=part_recv,
            device_id=target, device_id_type=MESH,
        ).start()
        return carry

    lax.fori_loop(1, devices, send, 0)
    recv[me] = part[me]
    others = pl.ds(0, devices - 1)
    pltpu.make_async_copy(part.at[others], part.at[others], part_send).wait()
    pltpu.make_async_copy(recv.at[others], recv.at[others], part_recv).wait()

    span = obs.shape[0]
    high_id = lax.broadcasted_iota(jnp.int32, (span, LANES), 0)
    low_id = lax.broadcasted_iota(jnp.int32, (LANES, LANES), 0)

    def gather_up(group, acc):
        left, right = [], []
        for i in range(GROUP):
            o = group * GROUP + i
            value = recv[o]
            target = owner[0, pl.ds(o, 1), :]
            top = value.astype(jnp.bfloat16).astype(jnp.float32)
            rest = value - top
            mid = rest.astype(jnp.bfloat16).astype(jnp.float32)
            pieces = (top, mid, rest - mid)
            hit = high_id == lax.shift_right_logical(target, 7)
            left.append(
                jnp.concatenate(
                    [jnp.where(hit, p, 0.0).astype(jnp.bfloat16) for p in pieces], axis=0
                )
            )
            right.append(
                jnp.where(low_id == (target & (LANES - 1)), 1.0, 0.0).astype(jnp.bfloat16)
            )
        return acc + lax.dot_general(
            jnp.concatenate(left, axis=1), jnp.concatenate(right, axis=1),
            (((1,), (1,)), ((), ())), preferred_element_type=jnp.float32,
        )

    acc = lax.fori_loop(
        0, devices // GROUP, gather_up, jnp.zeros((3 * span, LANES), jnp.float32)
    )
    obs[...] = acc[0:span] + (acc[span : 2 * span] + acc[2 * span : 3 * span])


def local(nx, ny, *args):
    inc = args[0]
    nfields, nlevels, rows, cols = inc.shape
    layers = nfields * nlevels
    total = layers + nlevels + 1
    high, wide = rows + 24, cols + LANES
    packed = -(-ITERS * total // 8) * 8
    devices = nx * ny
    vmem = pl.BlockSpec(memory_space=pltpu.VMEM)
    f32 = jnp.float32
    shapes = [
        (total, high, wide), (nlevels, high, wide), (nlevels, high, wide),
        (packed, cols), (packed, cols), (rows, LANES), (rows, LANES),
        (packed, cols), (packed, cols),
        (rows, LANES), (16, LANES), (16, LANES), (rows, LANES), (16, LANES), (16, LANES),
        (layers * rows * (cols // LANES), LANES), (devices, 1, LANES), (devices, 1, LANES),
    ]
    smoothed, obs = pl.pallas_call(
        functools.partial(kernel, nx, ny),
        out_shape=(
            jax.ShapeDtypeStruct(inc.shape, f32),
            jax.ShapeDtypeStruct((OBS_DEV // LANES, LANES), f32),
        ),
        in_specs=[vmem] * len(args),
        out_specs=(vmem, vmem),
        scratch_shapes=[pltpu.VMEM(s, f32) for s in shapes]
        + [
            pltpu.SemaphoreType.DMA((8,)), pltpu.SemaphoreType.DMA((8,)),
            pltpu.SemaphoreType.DMA, pltpu.SemaphoreType.DMA,
        ],
        compiler_params=pltpu.CompilerParams(
            collective_id=0, has_side_effects=True, vmem_limit_bytes=32 * 1024 * 1024
        ),
        name="smooth_and_observe",
    )(*args)
    return smoothed, obs.reshape(OBS_DEV)


def solution(mesh):
    return jax.shard_map(
        functools.partial(local, mesh.shape["gx"], mesh.shape["gy"]),
        mesh=mesh,
        in_specs=(
            P(None, None, "gy", "gx"),
            P(None, "gy", "gx"),
            P("gy", "gx"),
            P(("gx", "gy"), None, None, None, None),
            P(("gx", "gy"), None, None, None),
            P(("gx", "gy"), None, None),
            P(("gx", "gy"), None, None),
        ),
        out_specs=(P(None, None, "gy", "gx"), P(("gx", "gy"))),
        check_vma=False,
    )
```

```python
import functools

import jax
import jax.numpy as jnp
from jax import lax
from jax.experimental import pallas as pl
from jax.experimental.pallas import tpu as pltpu
from jax.sharding import PartitionSpec as P

ITERS = 10
OBS_DEV = 4096
LANES = 128
EDGE = 12
MESH = pl.DeviceIdType.MESH
GROUP = 8


def kernel(
    nx, ny, *refs
):
    inputs, (smoothed, obs), held = refs[:7], refs[7:9], refs[9:16]
    inc, dif, mask, cells, weights, counts, owner = held
    (
        ext, c_east, c_north, to_prev, to_next, first_cols, last_cols,
        from_prev, from_next, east_mid, east_next, east_prev, west_mid, west_next, west_prev,
        table, pieces, part, recv, load_sem, halo_send, halo_recv, part_send, part_recv,
    ) = refs[16:]
    loads = [
        pltpu.make_async_copy(src, dst, load_sem.at[i])
        for i, (src, dst) in enumerate(zip(inputs, held))
    ]
    for load in loads:
        load.start()
    nfields, nlevels, rows, cols = inc.shape
    layers = nfields * nlevels
    total = layers + nlevels + 1
    high, wide = ext.shape[1:]
    devices = nx * ny
    gx, gy = lax.axis_index("gx"), lax.axis_index("gy")
    me = gx * ny + gy

    def place(step):
        other = lax.rem(me + step, devices)
        return other, (lax.div(other, ny), lax.rem(other, ny))

    barrier = pltpu.get_barrier_semaphore()

    def greet(step, carry):
        pl.semaphore_signal(barrier, inc=1, device_id=place(step)[1], device_id_type=MESH)
        return carry

    lax.fori_loop(1, devices, greet, 0)

    for load in loads[:3]:
        load.wait()
    lane = lax.broadcasted_iota(jnp.int32, (rows, LANES), 1)
    wet = mask[...].astype(jnp.float32)
    packed_first = jnp.zeros((rows, LANES), jnp.float32)
    packed_last = jnp.zeros((rows, LANES), jnp.float32)
    for k in range(total):
        if k < layers:
            value = inc[k // nlevels, k % nlevels] * wet
        elif k < layers + nlevels:
            value = dif[k - layers]
        else:
            value = wet
        ext[k, 0:rows, 0:cols] = value
        ext[k, 32:40, 0:cols] = jnp.zeros((8, cols), jnp.float32)
        to_next[ITERS * k : ITERS * (k + 1), :] = value[rows - ITERS : rows]
        to_prev[ITERS * k : ITERS * (k + 1), :] = value[0:ITERS]
        here = (lane >= EDGE * k) & (lane < EDGE * (k + 1))
        first = value[:, 0:LANES]
        last = value[:, cols - LANES : cols]
        if k:
            first = pltpu.roll(first, EDGE * k, 1)
        last = pltpu.roll(last, (EDGE * k + EDGE) % LANES, 1)
        packed_first = jnp.where(here, first, packed_first)
        packed_last = jnp.where(here, last, packed_last)
    first_cols[...] = packed_first
    last_cols[...] = packed_last

    pl.semaphore_wait(barrier, devices - 1)

    east, west = lax.rem(gx + 1, nx), lax.rem(gx + nx - 1, nx)
    north, south = lax.rem(gy + 1, ny), lax.rem(gy + ny - 1, ny)
    plan = [
        (to_next, from_prev, (gx, north)),
        (to_prev, from_next, (gx, south)),
        (first_cols, east_mid, (west, gy)),
        (last_cols, west_mid, (east, gy)),
        (first_cols.at[0:16], east_next, (west, south)),
        (first_cols.at[8:24], east_prev, (west, north)),
        (last_cols.at[0:16], west_next, (east, south)),
        (last_cols.at[8:24], west_prev, (east, north)),
    ]
    copies = [
        pltpu.make_async_remote_copy(
            src_ref=src, dst_ref=dst, send_sem=halo_send.at[i], recv_sem=halo_recv.at[i],
            device_id=target, device_id_type=MESH,
        )
        for i, (src, dst, target) in enumerate(plan)
    ]
    for copy in copies:
        copy.start()

    for copy in copies[2:]:
        copy.wait_recv()
    sub = lax.broadcasted_iota(jnp.int32, (8, LANES), 0)
    lane48 = lax.broadcasted_iota(jnp.int32, (high, LANES), 1)

    def stack(mid, after, before):
        return jnp.concatenate(
            [mid[...], after[0:8], jnp.where(sub < 4, after[8:16], before[0:8]), before[8:16]], axis=0
        )

    east_all = stack(east_mid, east_next, east_prev)
    west_all = stack(west_mid, west_next, west_prev)
    for k in range(total):
        right = pltpu.roll(east_all, (LANES - EDGE * k) % LANES, 1) if k else east_all
        left = pltpu.roll(west_all, (2 * LANES - EDGE - EDGE * k) % LANES, 1)
        ext[k, :, cols:wide] = jnp.where(lane48 < LANES // 2, right, left)
    for copy in copies[:2]:
        copy.wait_recv()
    for k in range(total):
        ext[k, rows : rows + ITERS, 0:cols] = from_next[ITERS * k : ITERS * (k + 1), :]
        ext[k, high - ITERS : high, 0:cols] = from_prev[ITERS * k : ITERS * (k + 1), :]
    row_id = lax.broadcasted_iota(jnp.int32, (high, wide), 0)
    lowest = jnp.where(gy == 0, 36, high)
    highest = jnp.where(gy == ny - 1, rows, 36)
    outside = ((row_id >= highest) & (row_id < 36)) | (row_id >= lowest)
    wet_all = jnp.where(outside, 0.0, ext[total - 1])

    def up(array, axis):
        return pltpu.roll(array, array.shape[axis] - 1, axis)

    wet_east = wet_all * up(wet_all, 1)
    wet_north = wet_all * up(wet_all, 0)
    for level in range(nlevels):
        diffuse = ext[layers + level]
        c_east[level] = 0.5 * (diffuse + up(diffuse, 1)) * wet_east
        c_north[level] = 0.5 * (diffuse + up(diffuse, 0)) * wet_north
    for level in range(nlevels):

        def advance(_, fields):
            ce, cn = c_east[level], c_north[level]
            out = []
            for f in fields:
                flux_e = ce * (up(f, 1) - f)
                flux_n = cn * (up(f, 0) - f)
                f = f + (flux_e - pltpu.roll(flux_e, 1, 1)) + (flux_n - pltpu.roll(flux_n, 1, 0))
                out.append(f)
            return tuple(out)

        fields = lax.fori_loop(
            0, ITERS, advance, tuple(ext[f * nlevels + level] for f in range(nfields))
        )
        for f in range(nfields):
            k = f * nlevels + level
            smoothed[f, level] = fields[f][0:rows, 0:cols]
            table[k * rows : (k + 1) * rows, :] = fields[f][0:rows, 0:cols]
    for copy in copies:
        copy.wait_send()
    for load in loads[3:]:
        load.wait()

    lines = table.shape[0]
    whole = table[...]
    top = whole.astype(jnp.bfloat16)
    pieces[0:lines] = top
    pieces[lines : 2 * lines] = (whole - top.astype(jnp.float32)).astype(jnp.bfloat16)
    slot = lax.broadcasted_iota(jnp.int32, (8, LANES), 0)
    low16 = lax.broadcasted_iota(jnp.int32, (16, LANES), 0)
    steps = [(low16 + c).astype(jnp.float32).astype(jnp.bfloat16) for c in range(0, cols, 16)]
    one, none = jnp.ones((16, LANES), jnp.bfloat16), jnp.zeros((16, LANES), jnp.bfloat16)

    def look_up(o, carry):
        col = cells[0, o, 2]
        line = cells[0, o, 0] * rows + cells[0, o, 1]
        weight = jnp.where(slot < counts[0, pl.ds(o, 1), :], weights[0, o], 0.0)
        acc = jnp.zeros((8, LANES), jnp.float32)
        for k in range(0, 8, 2):
            hot = []
            for j in (k, k + 1):
                want = jnp.broadcast_to(col[j : j + 1], (16, LANES))
                want = want.astype(jnp.float32).astype(jnp.bfloat16)
                hot.append(
                    jnp.concatenate([jnp.where(s == want, one, none) for s in steps], axis=0)
                )
            found = jnp.dot(
                pieces[...], jnp.concatenate(hot, axis=1), preferred_element_type=jnp.float32
            )
            found = found[0:lines] + found[lines : 2 * lines]
            for i, j in enumerate((k, k + 1)):
                want = jnp.broadcast_to(line[j : j + 1], (8, LANES))
                tiles = [found[t : t + 8, i * LANES : (i + 1) * LANES] for t in range(0, lines, 8)]
                bit = 8
                while len(tiles) > 1:
                    odd = (want & bit) != 0
                    tiles = [
                        jnp.where(odd, tiles[t + 1], tiles[t]) if t + 1 < len(tiles) else tiles[t]
                        for t in range(0, len(tiles), 2)
                    ]
                    bit *= 2
                scale = jnp.broadcast_to(weight[j : j + 1], (8, LANES))
                acc = acc + jnp.where(slot == (want & 7), tiles[0], 0.0) * scale
        part[o] = jnp.sum(acc, axis=0, keepdims=True)
        return carry

    lax.fori_loop(0, devices, look_up, 0)

    def send(step, carry):
        other, target = place(step)
        pltpu.make_async_remote_copy(
            src_ref=part.at[other], dst_ref=recv.at[me], send_sem=part_send, recv_sem=part_recv,
            device_id=target, device_id_type=MESH,
        ).start()
        return carry

    lax.fori_loop(1, devices, send, 0)
    recv[me] = part[me]
    others = pl.ds(0, devices - 1)
    pltpu.make_async_copy(part.at[others], part.at[others], part_send).wait()
    pltpu.make_async_copy(recv.at[others], recv.at[others], part_recv).wait()

    span = obs.shape[0]
    high_id = lax.broadcasted_iota(jnp.int32, (span, LANES), 0)
    low_id = lax.broadcasted_iota(jnp.int32, (LANES, LANES), 0)

    def gather_up(group, acc):
        left, right = [], []
        for i in range(GROUP):
            o = group * GROUP + i
            value = recv[o]
            target = owner[0, pl.ds(o, 1), :]
            top = value.astype(jnp.bfloat16).astype(jnp.float32)
            rest = value - top
            mid = rest.astype(jnp.bfloat16).astype(jnp.float32)
            parts = (top, mid, rest - mid)
            hit = high_id == lax.shift_right_logical(target, 7)
            left.append(
                jnp.concatenate(
                    [jnp.where(hit, p, 0.0).astype(jnp.bfloat16) for p in parts], axis=0
                )
            )
            right.append(
                jnp.where(low_id == (target & (LANES - 1)), 1.0, 0.0).astype(jnp.bfloat16)
            )
        return acc + lax.dot_general(
            jnp.concatenate(left, axis=1), jnp.concatenate(right, axis=1),
            (((1,), (1,)), ((), ())), preferred_element_type=jnp.float32,
        )

    acc = lax.fori_loop(
        0, devices // GROUP, gather_up, jnp.zeros((3 * span, LANES), jnp.float32)
    )
    obs[...] = acc[0:span] + (acc[span : 2 * span] + acc[2 * span : 3 * span])


def local(nx, ny, *args):
    inc = args[0]
    nfields, nlevels, rows, cols = inc.shape
    layers = nfields * nlevels
    total = layers + nlevels + 1
    high, wide = rows + 24, cols + LANES
    packed = -(-ITERS * total // 8) * 8
    devices = nx * ny
    vmem = pl.BlockSpec(memory_space=pltpu.VMEM)
    f32 = jnp.float32
    shapes = [
        (total, high, wide), (nlevels, high, wide), (nlevels, high, wide),
        (packed, cols), (packed, cols), (rows, LANES), (rows, LANES),
        (packed, cols), (packed, cols),
        (rows, LANES), (16, LANES), (16, LANES), (rows, LANES), (16, LANES), (16, LANES),
        (layers * rows, cols),
    ]
    slots = pltpu.VMEM((devices, 1, LANES), f32)
    smoothed, obs = pl.pallas_call(
        functools.partial(kernel, nx, ny),
        out_shape=(
            jax.ShapeDtypeStruct(inc.shape, f32),
            jax.ShapeDtypeStruct((OBS_DEV // LANES, LANES), f32),
        ),
        in_specs=[pl.BlockSpec(memory_space=pl.ANY)] * len(args),
        out_specs=(vmem, vmem),
        scratch_shapes=[pltpu.VMEM(a.shape, a.dtype) for a in args]
        + [pltpu.VMEM(s, f32) for s in shapes]
        + [pltpu.VMEM((2 * layers * rows, cols), jnp.bfloat16), slots, slots]
        + [
            pltpu.SemaphoreType.DMA((len(args),)),
            pltpu.SemaphoreType.DMA((8,)), pltpu.SemaphoreType.DMA((8,)),
            pltpu.SemaphoreType.DMA, pltpu.SemaphoreType.DMA,
        ],
        compiler_params=pltpu.CompilerParams(
            collective_id=0, has_side_effects=True, vmem_limit_bytes=56 * 1024 * 1024
        ),
        name="smooth_and_observe",
    )(*args)
    return smoothed, obs.reshape(OBS_DEV)


def solution(mesh):
    return jax.shard_map(
        functools.partial(local, mesh.shape["gx"], mesh.shape["gy"]),
        mesh=mesh,
        in_specs=(
            P(None, None, "gy", "gx"),
            P(None, "gy", "gx"),
            P("gy", "gx"),
            P(("gx", "gy"), None, None, None, None),
            P(("gx", "gy"), None, None, None),
            P(("gx", "gy"), None, None),
            P(("gx", "gy"), None, None),
        ),
        out_specs=(P(None, None, "gy", "gx"), P(("gx", "gy"))),
        check_vma=False,
    )
```

```python
import functools

import jax
import jax.numpy as jnp
from jax import lax
from jax.experimental import pallas as pl
from jax.experimental.pallas import tpu as pltpu
from jax.sharding import PartitionSpec as P

ITERS = 10
OBS_DEV = 4096
LANES = 128
EDGE = 12
TOGETHER = 4
MESH = pl.DeviceIdType.MESH
GROUP = 8


def kernel(
    nx, ny, *refs
):
    inputs, (smoothed, obs), held = refs[:7], refs[7:9], refs[9:16]
    inc, dif, mask, cells, weights, counts, owner = held
    (
        ext, c_east, c_north, to_prev, to_next, first_cols, last_cols,
        from_prev, from_next, east_mid, east_next, east_prev, west_mid, west_next, west_prev,
        table, pieces, part, recv, load_sem, halo_send, halo_recv, part_send, part_recv,
    ) = refs[16:]
    loads = [
        pltpu.make_async_copy(src, dst, load_sem.at[i])
        for i, (src, dst) in enumerate(zip(inputs, held))
    ]
    for load in loads:
        load.start()
    nfields, nlevels, rows, cols = inc.shape
    layers = nfields * nlevels
    total = layers + nlevels + 1
    high, wide = ext.shape[1:]
    devices = nx * ny
    gx, gy = lax.axis_index("gx"), lax.axis_index("gy")
    me = gx * ny + gy

    def place(step):
        other = lax.rem(me + step, devices)
        return other, (lax.div(other, ny), lax.rem(other, ny))

    barrier = pltpu.get_barrier_semaphore()

    def greet(step, carry):
        pl.semaphore_signal(barrier, inc=1, device_id=place(step)[1], device_id_type=MESH)
        return carry

    lax.fori_loop(1, devices, greet, 0)

    for load in loads[:3]:
        load.wait()
    lane = lax.broadcasted_iota(jnp.int32, (rows, LANES), 1)
    wet = mask[...].astype(jnp.float32)
    packed_first = jnp.zeros((rows, LANES), jnp.float32)
    packed_last = jnp.zeros((rows, LANES), jnp.float32)
    for k in range(total):
        if k < layers:
            value = inc[k // nlevels, k % nlevels] * wet
        elif k < layers + nlevels:
            value = dif[k - layers]
        else:
            value = wet
        ext[k, 0:rows, 0:cols] = value
        ext[k, 32:40, 0:cols] = jnp.zeros((8, cols), jnp.float32)
        to_next[ITERS * k : ITERS * (k + 1), :] = value[rows - ITERS : rows]
        to_prev[ITERS * k : ITERS * (k + 1), :] = value[0:ITERS]
        here = (lane >= EDGE * k) & (lane < EDGE * (k + 1))
        first = value[:, 0:LANES]
        last = value[:, cols - LANES : cols]
        if k:
            first = pltpu.roll(first, EDGE * k, 1)
        last = pltpu.roll(last, (EDGE * k + EDGE) % LANES, 1)
        packed_first = jnp.where(here, first, packed_first)
        packed_last = jnp.where(here, last, packed_last)
    first_cols[...] = packed_first
    last_cols[...] = packed_last

    pl.semaphore_wait(barrier, devices - 1)

    east, west = lax.rem(gx + 1, nx), lax.rem(gx + nx - 1, nx)
    north, south = lax.rem(gy + 1, ny), lax.rem(gy + ny - 1, ny)
    plan = [
        (to_next, from_prev, (gx, north)),
        (to_prev, from_next, (gx, south)),
        (first_cols, east_mid, (west, gy)),
        (last_cols, west_mid, (east, gy)),
        (first_cols.at[0:16], east_next, (west, south)),
        (first_cols.at[8:24], east_prev, (west, north)),
        (last_cols.at[0:16], west_next, (east, south)),
        (last_cols.at[8:24], west_prev, (east, north)),
    ]
    copies = [
        pltpu.make_async_remote_copy(
            src_ref=src, dst_ref=dst, send_sem=halo_send.at[i], recv_sem=halo_recv.at[i],
            device_id=target, device_id_type=MESH,
        )
        for i, (src, dst, target) in enumerate(plan)
    ]
    for copy in copies:
        copy.start()

    for copy in copies[2:]:
        copy.wait_recv()
    sub = lax.broadcasted_iota(jnp.int32, (8, LANES), 0)
    lane48 = lax.broadcasted_iota(jnp.int32, (high, LANES), 1)

    def stack(mid, after, before):
        return jnp.concatenate(
            [mid[...], after[0:8], jnp.where(sub < 4, after[8:16], before[0:8]), before[8:16]], axis=0
        )

    east_all = stack(east_mid, east_next, east_prev)
    west_all = stack(west_mid, west_next, west_prev)
    for k in range(total):
        right = pltpu.roll(east_all, (LANES - EDGE * k) % LANES, 1) if k else east_all
        left = pltpu.roll(west_all, (2 * LANES - EDGE - EDGE * k) % LANES, 1)
        ext[k, :, cols:wide] = jnp.where(lane48 < LANES // 2, right, left)
    for copy in copies[:2]:
        copy.wait_recv()
    for k in range(total):
        ext[k, rows : rows + ITERS, 0:cols] = from_next[ITERS * k : ITERS * (k + 1), :]
        ext[k, high - ITERS : high, 0:cols] = from_prev[ITERS * k : ITERS * (k + 1), :]
    row_id = lax.broadcasted_iota(jnp.int32, (high, wide), 0)
    lowest = jnp.where(gy == 0, 36, high)
    highest = jnp.where(gy == ny - 1, rows, 36)
    outside = ((row_id >= highest) & (row_id < 36)) | (row_id >= lowest)
    wet_all = jnp.where(outside, 0.0, ext[total - 1])

    def up(array, axis):
        return pltpu.roll(array, array.shape[axis] - 1, axis)

    wet_east = wet_all * up(wet_all, 1)
    wet_north = wet_all * up(wet_all, 0)
    for level in range(nlevels):
        diffuse = ext[layers + level]
        c_east[level] = 0.5 * (diffuse + up(diffuse, 1)) * wet_east
        c_north[level] = 0.5 * (diffuse + up(diffuse, 0)) * wet_north
    for level in range(nlevels):

        def advance(_, fields):
            ce, cn = c_east[level], c_north[level]
            out = []
            for f in fields:
                flux_e = ce * (up(f, 1) - f)
                flux_n = cn * (up(f, 0) - f)
                f = f + (flux_e - pltpu.roll(flux_e, 1, 1)) + (flux_n - pltpu.roll(flux_n, 1, 0))
                out.append(f)
            return tuple(out)

        fields = lax.fori_loop(
            0, ITERS, advance, tuple(ext[f * nlevels + level] for f in range(nfields))
        )
        for f in range(nfields):
            k = f * nlevels + level
            smoothed[f, level] = fields[f][0:rows, 0:cols]
            table[k * rows : (k + 1) * rows, :] = fields[f][0:rows, 0:cols]
    for copy in copies:
        copy.wait_send()
    for load in loads[3:]:
        load.wait()

    lines = table.shape[0]
    whole = table[...]
    top = whole.astype(jnp.bfloat16)
    pieces[0:lines] = top
    pieces[lines : 2 * lines] = (whole - top.astype(jnp.float32)).astype(jnp.bfloat16)
    slot = lax.broadcasted_iota(jnp.int32, (8, LANES), 0)
    low16 = lax.broadcasted_iota(jnp.int32, (16, LANES), 0)
    steps = [(low16 + c).astype(jnp.float32).astype(jnp.bfloat16) for c in range(0, cols, 16)]
    one, none = jnp.ones((16, LANES), jnp.bfloat16), jnp.zeros((16, LANES), jnp.bfloat16)

    def look_up(o):
        col = cells[0, o, 2]
        line = cells[0, o, 0] * rows + cells[0, o, 1]
        weight = jnp.where(slot < counts[0, pl.ds(o, 1), :], weights[0, o], 0.0)
        acc = jnp.zeros((8, LANES), jnp.float32)
        for k in range(0, 8, 2):
            hot = []
            for j in (k, k + 1):
                want = jnp.broadcast_to(col[j : j + 1], (16, LANES))
                want = want.astype(jnp.float32).astype(jnp.bfloat16)
                hot.append(
                    jnp.concatenate([jnp.where(s == want, one, none) for s in steps], axis=0)
                )
            found = jnp.dot(
                pieces[...], jnp.concatenate(hot, axis=1), preferred_element_type=jnp.float32
            )
            found = found[0:lines] + found[lines : 2 * lines]
            for i, j in enumerate((k, k + 1)):
                want = jnp.broadcast_to(line[j : j + 1], (8, LANES))
                tiles = [found[t : t + 8, i * LANES : (i + 1) * LANES] for t in range(0, lines, 8)]
                bit = 8
                while len(tiles) > 1:
                    odd = (want & bit) != 0
                    tiles = [
                        jnp.where(odd, tiles[t + 1], tiles[t]) if t + 1 < len(tiles) else tiles[t]
                        for t in range(0, len(tiles), 2)
                    ]
                    bit *= 2
                scale = jnp.broadcast_to(weight[j : j + 1], (8, LANES))
                acc = acc + jnp.where(slot == (want & 7), tiles[0], 0.0) * scale
        part[o] = jnp.sum(acc, axis=0, keepdims=True)

    def send(other, target):
        pltpu.make_async_remote_copy(
            src_ref=part.at[other], dst_ref=recv.at[me], send_sem=part_send, recv_sem=part_recv,
            device_id=target, device_id_type=MESH,
        ).start()

    def several(group, carry):
        at = [place(group * TOGETHER + i) for i in range(TOGETHER)]
        for o, _ in at:
            look_up(o)
        for o, target in at:
            send(o, target)
        return carry

    lax.fori_loop(1, devices // TOGETHER, several, 0)
    at = [place(i) for i in range(TOGETHER)]
    for o, _ in at:
        look_up(o)
    for o, target in at[1:]:
        send(o, target)
    recv[me] = part[me]
    others = pl.ds(0, devices - 1)
    pltpu.make_async_copy(part.at[others], part.at[others], part_send).wait()
    pltpu.make_async_copy(recv.at[others], recv.at[others], part_recv).wait()

    span = obs.shape[0]
    high_id = lax.broadcasted_iota(jnp.int32, (span, LANES), 0)
    low_id = lax.broadcasted_iota(jnp.int32, (LANES, LANES), 0)

    def gather_up(group, acc):
        left, right = [], []
        for i in range(GROUP):
            o = group * GROUP + i
            value = recv[o]
            target = owner[0, pl.ds(o, 1), :]
            top = value.astype(jnp.bfloat16).astype(jnp.float32)
            rest = value - top
            mid = rest.astype(jnp.bfloat16).astype(jnp.float32)
            parts = (top, mid, rest - mid)
            hit = high_id == lax.shift_right_logical(target, 7)
            left.append(
                jnp.concatenate(
                    [jnp.where(hit, p, 0.0).astype(jnp.bfloat16) for p in parts], axis=0
                )
            )
            right.append(
                jnp.where(low_id == (target & (LANES - 1)), 1.0, 0.0).astype(jnp.bfloat16)
            )
        return acc + lax.dot_general(
            jnp.concatenate(left, axis=1), jnp.concatenate(right, axis=1),
            (((1,), (1,)), ((), ())), preferred_element_type=jnp.float32,
        )

    acc = lax.fori_loop(
        0, devices // GROUP, gather_up, jnp.zeros((3 * span, LANES), jnp.float32)
    )
    obs[...] = acc[0:span] + (acc[span : 2 * span] + acc[2 * span : 3 * span])


def local(nx, ny, *args):
    inc = args[0]
    nfields, nlevels, rows, cols = inc.shape
    layers = nfields * nlevels
    total = layers + nlevels + 1
    high, wide = rows + 24, cols + LANES
    packed = -(-ITERS * total // 8) * 8
    devices = nx * ny
    vmem = pl.BlockSpec(memory_space=pltpu.VMEM)
    f32 = jnp.float32
    shapes = [
        (total, high, wide), (nlevels, high, wide), (nlevels, high, wide),
        (packed, cols), (packed, cols), (rows, LANES), (rows, LANES),
        (packed, cols), (packed, cols),
        (rows, LANES), (16, LANES), (16, LANES), (rows, LANES), (16, LANES), (16, LANES),
        (layers * rows, cols),
    ]
    slots = pltpu.VMEM((devices, 1, LANES), f32)
    smoothed, obs = pl.pallas_call(
        functools.partial(kernel, nx, ny),
        out_shape=(
            jax.ShapeDtypeStruct(inc.shape, f32),
            jax.ShapeDtypeStruct((OBS_DEV // LANES, LANES), f32),
        ),
        in_specs=[pl.BlockSpec(memory_space=pltpu.HBM)] * len(args),
        out_specs=(vmem, vmem),
        scratch_shapes=[pltpu.VMEM(a.shape, a.dtype) for a in args]
        + [pltpu.VMEM(s, f32) for s in shapes]
        + [pltpu.VMEM((2 * layers * rows, cols), jnp.bfloat16), slots, slots]
        + [
            pltpu.SemaphoreType.DMA((len(args),)),
            pltpu.SemaphoreType.DMA((8,)), pltpu.SemaphoreType.DMA((8,)),
            pltpu.SemaphoreType.DMA, pltpu.SemaphoreType.DMA,
        ],
        compiler_params=pltpu.CompilerParams(
            collective_id=0, has_side_effects=True, vmem_limit_bytes=56 * 1024 * 1024
        ),
        name="smooth_and_observe",
    )(*args)
    return smoothed, obs.reshape(OBS_DEV)


def solution(mesh):
    return jax.shard_map(
        functools.partial(local, mesh.shape["gx"], mesh.shape["gy"]),
        mesh=mesh,
        in_specs=(
            P(None, None, "gy", "gx"),
            P(None, "gy", "gx"),
            P("gy", "gx"),
            P(("gx", "gy"), None, None, None, None),
            P(("gx", "gy"), None, None, None),
            P(("gx", "gy"), None, None),
            P(("gx", "gy"), None, None),
        ),
        out_specs=(P(None, None, "gy", "gx"), P(("gx", "gy"))),
        check_vma=False,
    )
```

```python
import functools

import jax
import jax.numpy as jnp
from jax import lax
from jax.experimental import pallas as pl
from jax.experimental.pallas import tpu as pltpu
from jax.sharding import PartitionSpec as P

ITERS = 10
OBS_DEV = 4096
LANES = 128
EDGE = 12
TOGETHER = 4
MESH = pl.DeviceIdType.MESH
GROUP = 8


def kernel(
    nx, ny, *refs
):
    inputs, (smoothed, obs), held = refs[:7], refs[7:9], refs[9:16]
    inc, dif, mask, cells, weights, counts, owner = held
    (
        ext, c_east, c_north, to_prev, to_next, first_cols, last_cols,
        from_prev, from_next, east_mid, east_next, east_prev, west_mid, west_next, west_prev,
        table, pieces, part, recv, load_sem, halo_send, halo_recv, part_send, part_recv,
    ) = refs[16:]
    loads = [
        pltpu.make_async_copy(src, dst, load_sem.at[i])
        for i, (src, dst) in enumerate(zip(inputs, held))
    ]
    for load in loads:
        load.start()
    nfields, nlevels, rows, cols = inc.shape
    layers = nfields * nlevels
    total = layers + nlevels + 1
    high, wide = ext.shape[1:]
    devices = nx * ny
    gx, gy = lax.axis_index("gx"), lax.axis_index("gy")
    me = gx * ny + gy

    def place(step):
        other = lax.rem(me + step, devices)
        return other, (lax.div(other, ny), lax.rem(other, ny))

    barrier = pltpu.get_barrier_semaphore()

    def greet(step, carry):
        pl.semaphore_signal(barrier, inc=1, device_id=place(step)[1], device_id_type=MESH)
        return carry

    lax.fori_loop(1, devices, greet, 0)

    for load in loads[:3]:
        load.wait()
    lane = lax.broadcasted_iota(jnp.int32, (rows, LANES), 1)
    wet = mask[...].astype(jnp.float32)
    packed_first = jnp.zeros((rows, LANES), jnp.float32)
    packed_last = jnp.zeros((rows, LANES), jnp.float32)
    for k in range(total):
        if k < layers:
            value = inc[k // nlevels, k % nlevels] * wet
        elif k < layers + nlevels:
            value = dif[k - layers]
        else:
            value = wet
        ext[k, 0:rows, 0:cols] = value
        ext[k, 32:40, 0:cols] = jnp.zeros((8, cols), jnp.float32)
        to_next[ITERS * k : ITERS * (k + 1), :] = value[rows - ITERS : rows]
        to_prev[ITERS * k : ITERS * (k + 1), :] = value[0:ITERS]
        here = (lane >= EDGE * k) & (lane < EDGE * (k + 1))
        first = value[:, 0:LANES]
        last = value[:, cols - LANES : cols]
        if k:
            first = pltpu.roll(first, EDGE * k, 1)
        last = pltpu.roll(last, (EDGE * k + EDGE) % LANES, 1)
        packed_first = jnp.where(here, first, packed_first)
        packed_last = jnp.where(here, last, packed_last)
    first_cols[...] = packed_first
    last_cols[...] = packed_last

    pl.semaphore_wait(barrier, devices - 1)

    east, west = lax.rem(gx + 1, nx), lax.rem(gx + nx - 1, nx)
    north, south = lax.rem(gy + 1, ny), lax.rem(gy + ny - 1, ny)
    plan = [
        (to_next, from_prev, (gx, north)),
        (to_prev, from_next, (gx, south)),
        (first_cols, east_mid, (west, gy)),
        (last_cols, west_mid, (east, gy)),
        (first_cols.at[0:16], east_next, (west, south)),
        (first_cols.at[8:24], east_prev, (west, north)),
        (last_cols.at[0:16], west_next, (east, south)),
        (last_cols.at[8:24], west_prev, (east, north)),
    ]
    copies = [
        pltpu.make_async_remote_copy(
            src_ref=src, dst_ref=dst, send_sem=halo_send.at[i], recv_sem=halo_recv.at[i],
            device_id=target, device_id_type=MESH,
        )
        for i, (src, dst, target) in enumerate(plan)
    ]
    for copy in copies:
        copy.start()

    for copy in copies[2:]:
        copy.wait_recv()
    sub = lax.broadcasted_iota(jnp.int32, (8, LANES), 0)
    lane48 = lax.broadcasted_iota(jnp.int32, (high, LANES), 1)

    def stack(mid, after, before):
        return jnp.concatenate(
            [mid[...], after[0:8], jnp.where(sub < 4, after[8:16], before[0:8]), before[8:16]], axis=0
        )

    east_all = stack(east_mid, east_next, east_prev)
    west_all = stack(west_mid, west_next, west_prev)
    for k in range(total):
        right = pltpu.roll(east_all, (LANES - EDGE * k) % LANES, 1) if k else east_all
        left = pltpu.roll(west_all, (2 * LANES - EDGE - EDGE * k) % LANES, 1)
        ext[k, :, cols:wide] = jnp.where(lane48 < LANES // 2, right, left)
    for copy in copies[:2]:
        copy.wait_recv()
    for k in range(total):
        ext[k, rows : rows + ITERS, 0:cols] = from_next[ITERS * k : ITERS * (k + 1), :]
        ext[k, high - ITERS : high, 0:cols] = from_prev[ITERS * k : ITERS * (k + 1), :]
    row_id = lax.broadcasted_iota(jnp.int32, (high, wide), 0)
    lowest = jnp.where(gy == 0, 36, high)
    highest = jnp.where(gy == ny - 1, rows, 36)
    outside = ((row_id >= highest) & (row_id < 36)) | (row_id >= lowest)
    wet_all = jnp.where(outside, 0.0, ext[total - 1])

    def up(array, axis):
        return pltpu.roll(array, array.shape[axis] - 1, axis)

    wet_east = wet_all * up(wet_all, 1)
    wet_north = wet_all * up(wet_all, 0)
    for level in range(nlevels):
        diffuse = ext[layers + level]
        c_east[level] = 0.5 * (diffuse + up(diffuse, 1)) * wet_east
        c_north[level] = 0.5 * (diffuse + up(diffuse, 0)) * wet_north

    def advance(_, carry):
        after = []
        for k in range(layers):
            f, ce, cn = ext[k], c_east[k % nlevels], c_north[k % nlevels]
            flux_e = ce * (up(f, 1) - f)
            flux_n = cn * (up(f, 0) - f)
            after.append(
                f + (flux_e - pltpu.roll(flux_e, 1, 1)) + (flux_n - pltpu.roll(flux_n, 1, 0))
            )
        for k in range(layers):
            ext[k] = after[k]
        return carry

    lax.fori_loop(0, ITERS, advance, 0)
    for k in range(layers):
        table[k // nlevels, k % nlevels] = ext[k, 0:rows, 0:cols]
    write = pltpu.make_async_copy(table, smoothed, load_sem.at[len(loads)])
    write.start()
    for copy in copies:
        copy.wait_send()
    for load in loads[3:]:
        load.wait()

    lines = layers * rows
    whole = table[...].reshape(lines, cols)
    top = whole.astype(jnp.bfloat16)
    rest = (whole - top.astype(jnp.float32)).astype(jnp.bfloat16)
    halves = cols // LANES
    for h in range(halves):
        pieces[h * lines : (h + 1) * lines, 0:LANES] = top[:, h * LANES : (h + 1) * LANES]
        pieces[h * lines : (h + 1) * lines, LANES:] = rest[:, h * LANES : (h + 1) * LANES]
    slot = lax.broadcasted_iota(jnp.int32, (8, LANES), 0)
    low16 = lax.broadcasted_iota(jnp.int32, (16, LANES), 0)
    steps = [(low16 + c).astype(jnp.float32).astype(jnp.bfloat16) for c in range(0, LANES, 16)]
    one, none = jnp.ones((16, LANES), jnp.bfloat16), jnp.zeros((16, LANES), jnp.bfloat16)

    def look_up(o):
        col = cells[0, o, 2] & (LANES - 1)
        half = lax.shift_right_logical(cells[0, o, 2], 7)
        line = cells[0, o, 0] * rows + cells[0, o, 1]
        weight = jnp.where(slot < counts[0, pl.ds(o, 1), :], weights[0, o], 0.0)
        acc = jnp.zeros((8, LANES), jnp.float32)
        for k in range(0, 8, 2):
            hot = []
            for j in (k, k + 1):
                want = jnp.broadcast_to(col[j : j + 1], (16, LANES))
                want = want.astype(jnp.float32).astype(jnp.bfloat16)
                one_hot = [jnp.where(s == want, one, none) for s in steps]
                hot.append(jnp.concatenate(one_hot + one_hot, axis=0))
            found = jnp.dot(
                pieces[...], jnp.concatenate(hot, axis=1), preferred_element_type=jnp.float32
            )
            for i, j in enumerate((k, k + 1)):
                want = jnp.broadcast_to(line[j : j + 1], (8, LANES))
                trees = []
                for h in range(halves):
                    tiles = [
                        found[h * lines + t : h * lines + t + 8, i * LANES : (i + 1) * LANES]
                        for t in range(0, lines, 8)
                    ]
                    bit = 8
                    while len(tiles) > 1:
                        odd = (want & bit) != 0
                        tiles = [
                            jnp.where(odd, tiles[t + 1], tiles[t]) if t + 1 < len(tiles) else tiles[t]
                            for t in range(0, len(tiles), 2)
                        ]
                        bit *= 2
                    trees += tiles
                side = jnp.broadcast_to(half[j : j + 1], (8, LANES))
                picked = trees[0]
                for h in range(1, halves):
                    picked = jnp.where(side == h, trees[h], picked)
                scale = jnp.broadcast_to(weight[j : j + 1], (8, LANES))
                acc = acc + jnp.where(slot == (want & 7), picked, 0.0) * scale
        part[o] = jnp.sum(acc, axis=0, keepdims=True)

    def send(other, target):
        pltpu.make_async_remote_copy(
            src_ref=part.at[other], dst_ref=recv.at[me], send_sem=part_send, recv_sem=part_recv,
            device_id=target, device_id_type=MESH,
        ).start()

    def several(group, carry):
        at = [place(group * TOGETHER + i) for i in range(TOGETHER)]
        for o, _ in at:
            look_up(o)
        for o, target in at:
            send(o, target)
        return carry

    lax.fori_loop(1, devices // TOGETHER, several, 0)
    at = [place(i) for i in range(TOGETHER)]
    for o, _ in at:
        look_up(o)
    for o, target in at[1:]:
        send(o, target)
    recv[me] = part[me]
    others = pl.ds(0, devices - 1)
    pltpu.make_async_copy(part.at[others], part.at[others], part_send).wait()
    pltpu.make_async_copy(recv.at[others], recv.at[others], part_recv).wait()

    span = obs.shape[0]
    high_id = lax.broadcasted_iota(jnp.int32, (span, LANES), 0)
    low_id = lax.broadcasted_iota(jnp.int32, (LANES, LANES), 0)

    def gather_up(group, acc):
        left, right = [], []
        for i in range(GROUP):
            o = group * GROUP + i
            value = recv[o]
            target = owner[0, pl.ds(o, 1), :]
            top = value.astype(jnp.bfloat16).astype(jnp.float32)
            rest = value - top
            mid = rest.astype(jnp.bfloat16).astype(jnp.float32)
            parts = (top, mid, rest - mid)
            hit = high_id == lax.shift_right_logical(target, 7)
            left.append(
                jnp.concatenate(
                    [jnp.where(hit, p, 0.0).astype(jnp.bfloat16) for p in parts], axis=0
                )
            )
            right.append(
                jnp.where(low_id == (target & (LANES - 1)), 1.0, 0.0).astype(jnp.bfloat16)
            )
        return acc + lax.dot_general(
            jnp.concatenate(left, axis=1), jnp.concatenate(right, axis=1),
            (((1,), (1,)), ((), ())), preferred_element_type=jnp.float32,
        )

    acc = lax.fori_loop(
        0, devices // GROUP, gather_up, jnp.zeros((3 * span, LANES), jnp.float32)
    )
    write.wait()
    obs[...] = acc[0:span] + (acc[span : 2 * span] + acc[2 * span : 3 * span])


def local(nx, ny, *args):
    inc = args[0]
    nfields, nlevels, rows, cols = inc.shape
    layers = nfields * nlevels
    total = layers + nlevels + 1
    high, wide = rows + 24, cols + LANES
    packed = -(-ITERS * total // 8) * 8
    devices = nx * ny
    vmem = pl.BlockSpec(memory_space=pltpu.VMEM)
    f32 = jnp.float32
    shapes = [
        (total, high, wide), (nlevels, high, wide), (nlevels, high, wide),
        (packed, cols), (packed, cols), (rows, LANES), (rows, LANES),
        (packed, cols), (packed, cols),
        (rows, LANES), (16, LANES), (16, LANES), (rows, LANES), (16, LANES), (16, LANES),
        inc.shape,
    ]
    slots = pltpu.VMEM((devices, 1, LANES), f32)
    smoothed, obs = pl.pallas_call(
        functools.partial(kernel, nx, ny),
        out_shape=(
            jax.ShapeDtypeStruct(inc.shape, f32),
            jax.ShapeDtypeStruct((OBS_DEV // LANES, LANES), f32),
        ),
        in_specs=[pl.BlockSpec(memory_space=pltpu.HBM)] * len(args),
        out_specs=(pl.BlockSpec(memory_space=pltpu.HBM), vmem),
        scratch_shapes=[pltpu.VMEM(a.shape, a.dtype) for a in args]
        + [pltpu.VMEM(s, f32) for s in shapes]
        + [pltpu.VMEM((layers * rows * (cols // LANES), 2 * LANES), jnp.bfloat16), slots, slots]
        + [
            pltpu.SemaphoreType.DMA((len(args) + 1,)),
            pltpu.SemaphoreType.DMA((8,)), pltpu.SemaphoreType.DMA((8,)),
            pltpu.SemaphoreType.DMA, pltpu.SemaphoreType.DMA,
        ],
        compiler_params=pltpu.CompilerParams(
            collective_id=0, has_side_effects=True, vmem_limit_bytes=56 * 1024 * 1024
        ),
        name="smooth_and_observe",
    )(*args)
    return smoothed, obs.reshape(OBS_DEV)


def solution(mesh):
    return jax.shard_map(
        functools.partial(local, mesh.shape["gx"], mesh.shape["gy"]),
        mesh=mesh,
        in_specs=(
            P(None, None, "gy", "gx"),
            P(None, "gy", "gx"),
            P("gy", "gx"),
            P(("gx", "gy"), None, None, None, None),
            P(("gx", "gy"), None, None, None),
            P(("gx", "gy"), None, None),
            P(("gx", "gy"), None, None),
        ),
        out_specs=(P(None, None, "gy", "gx"), P(("gx", "gy"))),
        check_vma=False,
    )
```

```python
import functools

import jax
import jax.numpy as jnp
from jax import lax
from jax.experimental import pallas as pl
from jax.experimental.pallas import tpu as pltpu
from jax.sharding import PartitionSpec as P

ITERS = 10
OBS_DEV = 4096
LANES = 128
EDGE = 12
TOGETHER = 4
MESH = pl.DeviceIdType.MESH
GROUP = 8


def kernel(
    nx, ny, *refs
):
    inputs, (smoothed, obs), held = refs[:7], refs[7:9], refs[9:16]
    inc, dif, mask, cells, weights, counts, owner = held
    (
        ext, c_east, c_north, to_prev, to_next, first_cols, last_cols,
        from_prev, from_next, east_mid, east_next, east_prev, west_mid, west_next, west_prev,
        table, pieces, part, recv, load_sem, halo_send, halo_recv, part_send, part_recv,
    ) = refs[16:]
    loads = [
        pltpu.make_async_copy(src, dst, load_sem.at[i])
        for i, (src, dst) in enumerate(zip(inputs, held))
    ]
    for load in loads:
        load.start()
    nfields, nlevels, rows, cols = inc.shape
    layers = nfields * nlevels
    total = layers + nlevels + 1
    high, wide = ext.shape[1:]
    devices = nx * ny
    gx, gy = lax.axis_index("gx"), lax.axis_index("gy")
    me = gx * ny + gy

    def place(step):
        other = lax.rem(me + step, devices)
        return other, (lax.div(other, ny), lax.rem(other, ny))

    barrier = pltpu.get_barrier_semaphore()

    def greet(step, carry):
        pl.semaphore_signal(barrier, inc=1, device_id=place(step)[1], device_id_type=MESH)
        return carry

    lax.fori_loop(1, devices, greet, 0)

    for load in loads[:3]:
        load.wait()
    lane = lax.broadcasted_iota(jnp.int32, (rows, LANES), 1)
    wet = mask[...].astype(jnp.float32)
    packed_first = jnp.zeros((rows, LANES), jnp.float32)
    packed_last = jnp.zeros((rows, LANES), jnp.float32)
    for k in range(total):
        if k < layers:
            value = inc[k // nlevels, k % nlevels] * wet
        elif k < layers + nlevels:
            value = dif[k - layers]
        else:
            value = wet
        ext[k, 0:rows, 0:cols] = value
        ext[k, 32:40, 0:cols] = jnp.zeros((8, cols), jnp.float32)
        to_next[ITERS * k : ITERS * (k + 1), :] = value[rows - ITERS : rows]
        to_prev[ITERS * k : ITERS * (k + 1), :] = value[0:ITERS]
        here = (lane >= EDGE * k) & (lane < EDGE * (k + 1))
        first = value[:, 0:LANES]
        last = value[:, cols - LANES : cols]
        if k:
            first = pltpu.roll(first, EDGE * k, 1)
        last = pltpu.roll(last, (EDGE * k + EDGE) % LANES, 1)
        packed_first = jnp.where(here, first, packed_first)
        packed_last = jnp.where(here, last, packed_last)
    first_cols[...] = packed_first
    last_cols[...] = packed_last

    pl.semaphore_wait(barrier, devices - 1)

    east, west = lax.rem(gx + 1, nx), lax.rem(gx + nx - 1, nx)
    north, south = lax.rem(gy + 1, ny), lax.rem(gy + ny - 1, ny)
    plan = [
        (to_next, from_prev, (gx, north)),
        (to_prev, from_next, (gx, south)),
        (first_cols, east_mid, (west, gy)),
        (last_cols, west_mid, (east, gy)),
        (first_cols.at[0:16], east_next, (west, south)),
        (first_cols.at[8:24], east_prev, (west, north)),
        (last_cols.at[0:16], west_next, (east, south)),
        (last_cols.at[8:24], west_prev, (east, north)),
    ]
    copies = [
        pltpu.make_async_remote_copy(
            src_ref=src, dst_ref=dst, send_sem=halo_send.at[i], recv_sem=halo_recv.at[i],
            device_id=target, device_id_type=MESH,
        )
        for i, (src, dst, target) in enumerate(plan)
    ]
    for copy in copies:
        copy.start()

    for copy in copies[2:]:
        copy.wait_recv()
    sub = lax.broadcasted_iota(jnp.int32, (8, LANES), 0)
    lane48 = lax.broadcasted_iota(jnp.int32, (high, LANES), 1)

    def stack(mid, after, before):
        return jnp.concatenate(
            [mid[...], after[0:8], jnp.where(sub < 4, after[8:16], before[0:8]), before[8:16]], axis=0
        )

    east_all = stack(east_mid, east_next, east_prev)
    west_all = stack(west_mid, west_next, west_prev)
    for k in range(total):
        right = pltpu.roll(east_all, (LANES - EDGE * k) % LANES, 1) if k else east_all
        left = pltpu.roll(west_all, (2 * LANES - EDGE - EDGE * k) % LANES, 1)
        ext[k, :, cols:wide] = jnp.where(lane48 < LANES // 2, right, left)
    for copy in copies[:2]:
        copy.wait_recv()
    for k in range(total):
        ext[k, rows : rows + ITERS, 0:cols] = from_next[ITERS * k : ITERS * (k + 1), :]
        ext[k, high - ITERS : high, 0:cols] = from_prev[ITERS * k : ITERS * (k + 1), :]
    row_id = lax.broadcasted_iota(jnp.int32, (high, wide), 0)
    lowest = jnp.where(gy == 0, 36, high)
    highest = jnp.where(gy == ny - 1, rows, 36)
    outside = ((row_id >= highest) & (row_id < 36)) | (row_id >= lowest)
    wet_all = jnp.where(outside, 0.0, ext[total - 1])

    def up(array, axis):
        return pltpu.roll(array, array.shape[axis] - 1, axis)

    wet_east = wet_all * up(wet_all, 1)
    wet_north = wet_all * up(wet_all, 0)
    for level in range(nlevels):
        diffuse = ext[layers + level]
        c_east[level] = 0.5 * (diffuse + up(diffuse, 1)) * wet_east
        c_north[level] = 0.5 * (diffuse + up(diffuse, 0)) * wet_north

    def advance(_, carry):
        after = []
        for k in range(layers):
            f, ce, cn = ext[k], c_east[k % nlevels], c_north[k % nlevels]
            flux_e = ce * (up(f, 1) - f)
            flux_n = cn * (up(f, 0) - f)
            after.append(
                f + (flux_e - pltpu.roll(flux_e, 1, 1)) + (flux_n - pltpu.roll(flux_n, 1, 0))
            )
        for k in range(layers):
            ext[k] = after[k]
        return carry

    lax.fori_loop(0, ITERS, advance, 0)
    for k in range(layers):
        table[k // nlevels, k % nlevels] = ext[k, 0:rows, 0:cols]
    write = pltpu.make_async_copy(table, smoothed, load_sem.at[len(loads)])
    write.start()
    for copy in copies:
        copy.wait_send()
    for load in loads[3:]:
        load.wait()

    lines = layers * rows
    whole = table[...].reshape(lines, cols)
    top = whole.astype(jnp.bfloat16)
    rest = (whole - top.astype(jnp.float32)).astype(jnp.bfloat16)
    halves = cols // LANES
    for h in range(halves):
        pieces[h * lines : (h + 1) * lines, 0:LANES] = top[:, h * LANES : (h + 1) * LANES]
        pieces[h * lines : (h + 1) * lines, LANES:] = rest[:, h * LANES : (h + 1) * LANES]
    slot = lax.broadcasted_iota(jnp.int32, (8, LANES), 0)
    low16 = lax.broadcasted_iota(jnp.int32, (16, LANES), 0)
    steps = [(low16 + c).astype(jnp.float32).astype(jnp.bfloat16) for c in range(0, LANES, 16)]
    one, none = jnp.ones((16, LANES), jnp.bfloat16), jnp.zeros((16, LANES), jnp.bfloat16)

    def product(col, k):
        hot = []
        for j in (k, k + 1):
            want = jnp.broadcast_to(col[j : j + 1], (16, LANES))
            want = want.astype(jnp.float32).astype(jnp.bfloat16)
            one_hot = [jnp.where(s == want, one, none) for s in steps]
            hot.append(jnp.concatenate(one_hot + one_hot, axis=0))
        return jnp.dot(
            pieces[...], jnp.concatenate(hot, axis=1), preferred_element_type=jnp.float32
        )

    def select(found, acc, line, half, weight, k):
        for i, j in enumerate((k, k + 1)):
            want = jnp.broadcast_to(line[j : j + 1], (8, LANES))
            trees = []
            for h in range(halves):
                tiles = [
                    found[h * lines + t : h * lines + t + 8, i * LANES : (i + 1) * LANES]
                    for t in range(0, lines, 8)
                ]
                bit = 8
                while len(tiles) > 1:
                    odd = (want & bit) != 0
                    tiles = [
                        jnp.where(odd, tiles[t + 1], tiles[t]) if t + 1 < len(tiles) else tiles[t]
                        for t in range(0, len(tiles), 2)
                    ]
                    bit *= 2
                trees += tiles
            side = jnp.broadcast_to(half[j : j + 1], (8, LANES))
            picked = trees[0]
            for h in range(1, halves):
                picked = jnp.where(side == h, trees[h], picked)
            scale = jnp.broadcast_to(weight[j : j + 1], (8, LANES))
            acc = acc + jnp.where(slot == (want & 7), picked, 0.0) * scale
        return acc

    def look_up(owners):
        waiting = None
        sums = {}
        for n, o in enumerate(owners):
            col = cells[0, o, 2] & (LANES - 1)
            half = lax.shift_right_logical(cells[0, o, 2], 7)
            line = cells[0, o, 0] * rows + cells[0, o, 1]
            weight = jnp.where(slot < counts[0, pl.ds(o, 1), :], weights[0, o], 0.0)
            sums[n] = jnp.zeros((8, LANES), jnp.float32)
            for k in range(0, 8, 2):
                found = product(col, k)
                if waiting is not None:
                    m, args = waiting
                    sums[m] = select(args[0], sums[m], *args[1:])
                waiting = (n, (found, line, half, weight, k))
        m, args = waiting
        sums[m] = select(args[0], sums[m], *args[1:])
        for n, o in enumerate(owners):
            part[o] = jnp.sum(sums[n], axis=0, keepdims=True)

    def send(other, target):
        pltpu.make_async_remote_copy(
            src_ref=part.at[other], dst_ref=recv.at[me], send_sem=part_send, recv_sem=part_recv,
            device_id=target, device_id_type=MESH,
        ).start()

    def several(group, carry):
        at = [place(group * TOGETHER + i) for i in range(TOGETHER)]
        look_up([o for o, _ in at])
        for o, target in at:
            send(o, target)
        return carry

    lax.fori_loop(1, devices // TOGETHER, several, 0)
    at = [place(i) for i in range(TOGETHER)]
    look_up([o for o, _ in at])
    for o, target in at[1:]:
        send(o, target)
    recv[me] = part[me]
    others = pl.ds(0, devices - 1)
    pltpu.make_async_copy(part.at[others], part.at[others], part_send).wait()
    pltpu.make_async_copy(recv.at[others], recv.at[others], part_recv).wait()

    span = obs.shape[0]
    high_id = lax.broadcasted_iota(jnp.int32, (span, LANES), 0)
    low_id = lax.broadcasted_iota(jnp.int32, (LANES, LANES), 0)

    def gather_up(group, acc):
        left, right = [], []
        for i in range(GROUP):
            o = group * GROUP + i
            value = recv[o]
            target = owner[0, pl.ds(o, 1), :]
            top = value.astype(jnp.bfloat16).astype(jnp.float32)
            rest = value - top
            mid = rest.astype(jnp.bfloat16).astype(jnp.float32)
            parts = (top, mid, rest - mid)
            hit = high_id == lax.shift_right_logical(target, 7)
            left.append(
                jnp.concatenate(
                    [jnp.where(hit, p, 0.0).astype(jnp.bfloat16) for p in parts], axis=0
                )
            )
            right.append(
                jnp.where(low_id == (target & (LANES - 1)), 1.0, 0.0).astype(jnp.bfloat16)
            )
        return acc + lax.dot_general(
            jnp.concatenate(left, axis=1), jnp.concatenate(right, axis=1),
            (((1,), (1,)), ((), ())), preferred_element_type=jnp.float32,
        )

    acc = lax.fori_loop(
        0, devices // GROUP, gather_up, jnp.zeros((3 * span, LANES), jnp.float32), unroll=2
    )
    write.wait()
    obs[...] = acc[0:span] + (acc[span : 2 * span] + acc[2 * span : 3 * span])


def local(nx, ny, *args):
    inc = args[0]
    nfields, nlevels, rows, cols = inc.shape
    layers = nfields * nlevels
    total = layers + nlevels + 1
    high, wide = rows + 24, cols + LANES
    packed = -(-ITERS * total // 8) * 8
    devices = nx * ny
    vmem = pl.BlockSpec(memory_space=pltpu.VMEM)
    f32 = jnp.float32
    shapes = [
        (total, high, wide), (nlevels, high, wide), (nlevels, high, wide),
        (packed, cols), (packed, cols), (rows, LANES), (rows, LANES),
        (packed, cols), (packed, cols),
        (rows, LANES), (16, LANES), (16, LANES), (rows, LANES), (16, LANES), (16, LANES),
        inc.shape,
    ]
    slots = pltpu.VMEM((devices, 1, LANES), f32)
    smoothed, obs = pl.pallas_call(
        functools.partial(kernel, nx, ny),
        out_shape=(
            jax.ShapeDtypeStruct(inc.shape, f32),
            jax.ShapeDtypeStruct((OBS_DEV // LANES, LANES), f32),
        ),
        in_specs=[pl.BlockSpec(memory_space=pltpu.HBM)] * len(args),
        out_specs=(pl.BlockSpec(memory_space=pltpu.HBM), vmem),
        scratch_shapes=[pltpu.VMEM(a.shape, a.dtype) for a in args]
        + [pltpu.VMEM(s, f32) for s in shapes]
        + [pltpu.VMEM((layers * rows * (cols // LANES), 2 * LANES), jnp.bfloat16), slots, slots]
        + [
            pltpu.SemaphoreType.DMA((len(args) + 1,)),
            pltpu.SemaphoreType.DMA((8,)), pltpu.SemaphoreType.DMA((8,)),
            pltpu.SemaphoreType.DMA, pltpu.SemaphoreType.DMA,
        ],
        compiler_params=pltpu.CompilerParams(
            collective_id=0, has_side_effects=True, vmem_limit_bytes=56 * 1024 * 1024
        ),
        name="smooth_and_observe",
    )(*args)
    return smoothed, obs.reshape(OBS_DEV)


def solution(mesh):
    return jax.shard_map(
        functools.partial(local, mesh.shape["gx"], mesh.shape["gy"]),
        mesh=mesh,
        in_specs=(
            P(None, None, "gy", "gx"),
            P(None, "gy", "gx"),
            P("gy", "gx"),
            P(("gx", "gy"), None, None, None, None),
            P(("gx", "gy"), None, None, None),
            P(("gx", "gy"), None, None),
            P(("gx", "gy"), None, None),
        ),
        out_specs=(P(None, None, "gy", "gx"), P(("gx", "gy"))),
        check_vma=False,
    )
```

```python
import functools

import jax
import jax.numpy as jnp
from jax import lax
from jax.experimental import pallas as pl
from jax.experimental.pallas import tpu as pltpu
from jax.sharding import PartitionSpec as P

ITERS = 10
OBS_DEV = 4096
LANES = 128
EDGE = 12
TOGETHER = 4
MESH = pl.DeviceIdType.MESH
GROUP = 8


def kernel(
    nx, ny, *refs
):
    inputs, (smoothed, obs), held = refs[:7], refs[7:9], refs[9:16]
    inc, dif, mask, cells, weights, counts, owner = held
    (
        ext, c_east, c_north, to_prev, to_next, first_cols, last_cols,
        from_prev, from_next, east_mid, east_next, east_prev, west_mid, west_next, west_prev,
        table, pieces, low_hot, part, recv, load_sem, halo_send, halo_recv, part_send, part_recv,
    ) = refs[16:]
    loads = [
        pltpu.make_async_copy(src, dst, load_sem.at[i])
        for i, (src, dst) in enumerate(zip(inputs, held))
    ]
    for load in loads:
        load.start()
    nfields, nlevels, rows, cols = inc.shape
    layers = nfields * nlevels
    total = layers + nlevels + 1
    high, wide = ext.shape[1:]
    devices = nx * ny
    gx, gy = lax.axis_index("gx"), lax.axis_index("gy")
    me = gx * ny + gy

    def place(step):
        other = lax.rem(me + step, devices)
        return other, (lax.div(other, ny), lax.rem(other, ny))

    barrier = pltpu.get_barrier_semaphore()

    def greet(step, carry):
        pl.semaphore_signal(barrier, inc=1, device_id=place(step)[1], device_id_type=MESH)
        return carry

    lax.fori_loop(1, devices, greet, 0)

    for load in loads[:3]:
        load.wait()
    lane = lax.broadcasted_iota(jnp.int32, (rows, LANES), 1)
    wet = mask[...].astype(jnp.float32)
    for k in range(total):
        if k < layers:
            value = inc[k // nlevels, k % nlevels] * wet
        elif k < layers + nlevels:
            value = dif[k - layers]
        else:
            value = wet
        ext[k, 0:rows, 0:cols] = value
        ext[k, 32:40, 0:cols] = jnp.zeros((8, cols), jnp.float32)
        to_next[ITERS * k : ITERS * (k + 1), :] = value[rows - ITERS : rows]
        to_prev[ITERS * k : ITERS * (k + 1), :] = value[0:ITERS]

    pl.semaphore_wait(barrier, devices - 1)

    east, west = lax.rem(gx + 1, nx), lax.rem(gx + nx - 1, nx)
    north, south = lax.rem(gy + 1, ny), lax.rem(gy + ny - 1, ny)
    plan = [
        (to_next, from_prev, (gx, north)),
        (to_prev, from_next, (gx, south)),
        (first_cols, east_mid, (west, gy)),
        (last_cols, west_mid, (east, gy)),
        (first_cols.at[0:16], east_next, (west, south)),
        (first_cols.at[8:24], east_prev, (west, north)),
        (last_cols.at[0:16], west_next, (east, south)),
        (last_cols.at[8:24], west_prev, (east, north)),
    ]
    copies = [
        pltpu.make_async_remote_copy(
            src_ref=src, dst_ref=dst, send_sem=halo_send.at[i], recv_sem=halo_recv.at[i],
            device_id=target, device_id_type=MESH,
        )
        for i, (src, dst, target) in enumerate(plan)
    ]
    for copy in copies[:2]:
        copy.start()
    packed_first = jnp.zeros((rows, LANES), jnp.float32)
    packed_last = jnp.zeros((rows, LANES), jnp.float32)
    for k in range(total):
        value = ext[k, 0:rows, 0:cols]
        here = (lane >= EDGE * k) & (lane < EDGE * (k + 1))
        first = value[:, 0:LANES]
        last = value[:, cols - LANES : cols]
        if k:
            first = pltpu.roll(first, EDGE * k, 1)
        last = pltpu.roll(last, (EDGE * k + EDGE) % LANES, 1)
        packed_first = jnp.where(here, first, packed_first)
        packed_last = jnp.where(here, last, packed_last)
    first_cols[...] = packed_first
    last_cols[...] = packed_last
    for copy in copies[2:]:
        copy.start()

    loads[6].wait()
    low_id = lax.broadcasted_iota(jnp.int32, (LANES, LANES), 0)

    def mark(o, carry):
        low = owner[0, pl.ds(o, 1), :] & (LANES - 1)
        low_hot[o] = jnp.where(low_id == low, 1.0, 0.0).astype(jnp.bfloat16)
        return carry

    lax.fori_loop(0, devices, mark, 0, unroll=2)

    for copy in copies[2:]:
        copy.wait_recv()
    sub = lax.broadcasted_iota(jnp.int32, (8, LANES), 0)
    lane48 = lax.broadcasted_iota(jnp.int32, (high, LANES), 1)

    def stack(mid, after, before):
        return jnp.concatenate(
            [mid[...], after[0:8], jnp.where(sub < 4, after[8:16], before[0:8]), before[8:16]], axis=0
        )

    east_all = stack(east_mid, east_next, east_prev)
    west_all = stack(west_mid, west_next, west_prev)
    for k in range(total):
        right = pltpu.roll(east_all, (LANES - EDGE * k) % LANES, 1) if k else east_all
        left = pltpu.roll(west_all, (2 * LANES - EDGE - EDGE * k) % LANES, 1)
        ext[k, :, cols:wide] = jnp.where(lane48 < LANES // 2, right, left)
    for copy in copies[:2]:
        copy.wait_recv()
    for k in range(total):
        ext[k, rows : rows + ITERS, 0:cols] = from_next[ITERS * k : ITERS * (k + 1), :]
        ext[k, high - ITERS : high, 0:cols] = from_prev[ITERS * k : ITERS * (k + 1), :]
    row_id = lax.broadcasted_iota(jnp.int32, (high, wide), 0)
    lowest = jnp.where(gy == 0, 36, high)
    highest = jnp.where(gy == ny - 1, rows, 36)
    outside = ((row_id >= highest) & (row_id < 36)) | (row_id >= lowest)
    wet_all = jnp.where(outside, 0.0, ext[total - 1])

    def up(array, axis):
        return pltpu.roll(array, array.shape[axis] - 1, axis)

    wet_east = wet_all * up(wet_all, 1)
    wet_north = wet_all * up(wet_all, 0)
    for level in range(nlevels):
        diffuse = ext[layers + level]
        c_east[level] = 0.5 * (diffuse + up(diffuse, 1)) * wet_east
        c_north[level] = 0.5 * (diffuse + up(diffuse, 0)) * wet_north

    def advance(_, carry):
        after = []
        for k in range(layers):
            f, ce, cn = ext[k], c_east[k % nlevels], c_north[k % nlevels]
            flux_e = ce * (up(f, 1) - f)
            flux_n = cn * (up(f, 0) - f)
            after.append(
                f + (flux_e - pltpu.roll(flux_e, 1, 1)) + (flux_n - pltpu.roll(flux_n, 1, 0))
            )
        for k in range(layers):
            ext[k] = after[k]
        return carry

    lax.fori_loop(0, ITERS, advance, 0)
    for k in range(layers):
        table[k // nlevels, k % nlevels] = ext[k, 0:rows, 0:cols]
    write = pltpu.make_async_copy(table, smoothed, load_sem.at[len(loads)])
    write.start()
    for copy in copies:
        copy.wait_send()
    for load in loads[3:6]:
        load.wait()

    lines = layers * rows
    whole = table[...].reshape(lines, cols)
    top = whole.astype(jnp.bfloat16)
    rest = (whole - top.astype(jnp.float32)).astype(jnp.bfloat16)
    halves = cols // LANES
    for h in range(halves):
        pieces[h * lines : (h + 1) * lines, 0:LANES] = top[:, h * LANES : (h + 1) * LANES]
        pieces[h * lines : (h + 1) * lines, LANES:] = rest[:, h * LANES : (h + 1) * LANES]
    slot = lax.broadcasted_iota(jnp.int32, (8, LANES), 0)
    low16 = lax.broadcasted_iota(jnp.int32, (16, LANES), 0)
    steps = [(low16 + c).astype(jnp.float32).astype(jnp.bfloat16) for c in range(0, LANES, 16)]
    one, none = jnp.ones((16, LANES), jnp.bfloat16), jnp.zeros((16, LANES), jnp.bfloat16)

    def product(col, k):
        hot = []
        for j in (k, k + 1):
            want = jnp.broadcast_to(col[j : j + 1], (16, LANES))
            want = want.astype(jnp.float32).astype(jnp.bfloat16)
            one_hot = [jnp.where(s == want, one, none) for s in steps]
            hot.append(jnp.concatenate(one_hot + one_hot, axis=0))
        return jnp.dot(
            pieces[...], jnp.concatenate(hot, axis=1), preferred_element_type=jnp.float32
        )

    def select(found, acc, line, half, weight, k):
        for i, j in enumerate((k, k + 1)):
            want = jnp.broadcast_to(line[j : j + 1], (8, LANES))
            trees = []
            for h in range(halves):
                tiles = [
                    found[h * lines + t : h * lines + t + 8, i * LANES : (i + 1) * LANES]
                    for t in range(0, lines, 8)
                ]
                bit = 8
                while len(tiles) > 1:
                    odd = (want & bit) != 0
                    tiles = [
                        jnp.where(odd, tiles[t + 1], tiles[t]) if t + 1 < len(tiles) else tiles[t]
                        for t in range(0, len(tiles), 2)
                    ]
                    bit *= 2
                trees += tiles
            side = jnp.broadcast_to(half[j : j + 1], (8, LANES))
            picked = trees[0]
            for h in range(1, halves):
                picked = jnp.where(side == h, trees[h], picked)
            scale = jnp.broadcast_to(weight[j : j + 1], (8, LANES))
            acc = acc + jnp.where(slot == (want & 7), picked, 0.0) * scale
        return acc

    def look_up(owners):
        waiting = None
        sums = {}
        for n, o in enumerate(owners):
            col = cells[0, o, 2] & (LANES - 1)
            half = lax.shift_right_logical(cells[0, o, 2], 7)
            line = cells[0, o, 0] * rows + cells[0, o, 1]
            weight = jnp.where(slot < counts[0, pl.ds(o, 1), :], weights[0, o], 0.0)
            sums[n] = jnp.zeros((8, LANES), jnp.float32)
            for k in range(0, 8, 2):
                found = product(col, k)
                if waiting is not None:
                    m, args = waiting
                    sums[m] = select(args[0], sums[m], *args[1:])
                waiting = (n, (found, line, half, weight, k))
        m, args = waiting
        sums[m] = select(args[0], sums[m], *args[1:])
        for n, o in enumerate(owners):
            part[o] = jnp.sum(sums[n], axis=0, keepdims=True)

    def send(other, target):
        pltpu.make_async_remote_copy(
            src_ref=part.at[other], dst_ref=recv.at[me], send_sem=part_send, recv_sem=part_recv,
            device_id=target, device_id_type=MESH,
        ).start()

    def several(group, carry):
        at = [place(group * TOGETHER + i) for i in range(TOGETHER)]
        look_up([o for o, _ in at])
        for o, target in at:
            send(o, target)
        return carry

    lax.fori_loop(1, devices // TOGETHER, several, 0)
    at = [place(i) for i in range(TOGETHER)]
    look_up([o for o, _ in at])
    for o, target in at[1:]:
        send(o, target)
    recv[me] = part[me]
    others = pl.ds(0, devices - 1)
    pltpu.make_async_copy(part.at[others], part.at[others], part_send).wait()
    pltpu.make_async_copy(recv.at[others], recv.at[others], part_recv).wait()

    span = obs.shape[0]
    high_id = lax.broadcasted_iota(jnp.int32, (span, LANES), 0)

    def gather_up(group, acc):
        left, right = [], []
        for i in range(GROUP):
            o = group * GROUP + i
            value = recv[o]
            target = owner[0, pl.ds(o, 1), :]
            top = value.astype(jnp.bfloat16).astype(jnp.float32)
            rest = value - top
            mid = rest.astype(jnp.bfloat16).astype(jnp.float32)
            parts = (top, mid, rest - mid)
            hit = high_id == lax.shift_right_logical(target, 7)
            left.append(
                jnp.concatenate(
                    [jnp.where(hit, p, 0.0).astype(jnp.bfloat16) for p in parts], axis=0
                )
            )
            right.append(low_hot[o])
        return acc + lax.dot_general(
            jnp.concatenate(left, axis=1), jnp.concatenate(right, axis=1),
            (((1,), (1,)), ((), ())), preferred_element_type=jnp.float32,
        )

    acc = lax.fori_loop(
        0, devices // GROUP, gather_up, jnp.zeros((3 * span, LANES), jnp.float32), unroll=2
    )
    write.wait()
    obs[...] = acc[0:span] + (acc[span : 2 * span] + acc[2 * span : 3 * span])


def local(nx, ny, *args):
    inc = args[0]
    nfields, nlevels, rows, cols = inc.shape
    layers = nfields * nlevels
    total = layers + nlevels + 1
    high, wide = rows + 24, cols + LANES
    packed = -(-ITERS * total // 8) * 8
    devices = nx * ny
    vmem = pl.BlockSpec(memory_space=pltpu.VMEM)
    f32 = jnp.float32
    shapes = [
        (total, high, wide), (nlevels, high, wide), (nlevels, high, wide),
        (packed, cols), (packed, cols), (rows, LANES), (rows, LANES),
        (packed, cols), (packed, cols),
        (rows, LANES), (16, LANES), (16, LANES), (rows, LANES), (16, LANES), (16, LANES),
        inc.shape,
    ]
    slots = pltpu.VMEM((devices, 1, LANES), f32)
    smoothed, obs = pl.pallas_call(
        functools.partial(kernel, nx, ny),
        out_shape=(
            jax.ShapeDtypeStruct(inc.shape, f32),
            jax.ShapeDtypeStruct((OBS_DEV // LANES, LANES), f32),
        ),
        in_specs=[pl.BlockSpec(memory_space=pltpu.HBM)] * len(args),
        out_specs=(pl.BlockSpec(memory_space=pltpu.HBM), vmem),
        scratch_shapes=[pltpu.VMEM(a.shape, a.dtype) for a in args]
        + [pltpu.VMEM(s, f32) for s in shapes]
        + [pltpu.VMEM((layers * rows * (cols // LANES), 2 * LANES), jnp.bfloat16)]
        + [pltpu.VMEM((devices, LANES, LANES), jnp.bfloat16), slots, slots]
        + [
            pltpu.SemaphoreType.DMA((len(args) + 1,)),
            pltpu.SemaphoreType.DMA((8,)), pltpu.SemaphoreType.DMA((8,)),
            pltpu.SemaphoreType.DMA, pltpu.SemaphoreType.DMA,
        ],
        compiler_params=pltpu.CompilerParams(
            collective_id=0, has_side_effects=True, vmem_limit_bytes=56 * 1024 * 1024
        ),
        name="smooth_and_observe",
    )(*args)
    return smoothed, obs.reshape(OBS_DEV)


def solution(mesh):
    return jax.shard_map(
        functools.partial(local, mesh.shape["gx"], mesh.shape["gy"]),
        mesh=mesh,
        in_specs=(
            P(None, None, "gy", "gx"),
            P(None, "gy", "gx"),
            P("gy", "gx"),
            P(("gx", "gy"), None, None, None, None),
            P(("gx", "gy"), None, None, None),
            P(("gx", "gy"), None, None),
            P(("gx", "gy"), None, None),
        ),
        out_specs=(P(None, None, "gy", "gx"), P(("gx", "gy"))),
        check_vma=False,
    )
```
